512 devices in a mesh: tm: 16 (over z, core), space: 32 (over y, x).
Axes of the slice: x: 4, y: 8, z: 8, core: 2. Of those that a mesh axis runs over, the one named last changes fastest.
Arguments:
- thermal_anomaly_matrix: float32 [512, 393216], P('tm', 'space'), may hold values from -40 to 40
- filter_weights: float32 [31], replicated, may hold values from -0.12 to 1.2
Outputs:
- lower_factor: float32 [512, 512], replicated
- basis: float32 [512, 32, 12288], P(None, 'space', 'tm')
The draws below stay inside these ranges and needn't reach their ends.
All inputs are finite; a program needn't handle non-finite values.
Results may differ from the reference program's by a relative error of at most 0.000078.
Values sent between devices are 32-bit elements; how exact they have to be, the bound alone decides.
A program may use at most 64 MiB of HBM per device.

```python
import math
import jax
import jax.numpy as jnp
from jax import lax

TIME = 512
TAPS = 31
SPAN = 12288
GROUPS = 32
POINTS = 393216


def draw_thermal_anomaly_matrix(key, part):
    key = jax.random.fold_in(key, 11)
    first, second, third = jax.random.split(key, 3)
    time_scale = jnp.exp(jax.random.uniform(first, (TIME, 1), jnp.float32, 0.0, 0.5 * math.log(10.0)))
    point_scale = jnp.exp(jax.random.uniform(second, (1, POINTS), jnp.float32, 0.0, 0.5 * math.log(10.0)))
    base = jnp.clip(jax.random.normal(third, (TIME, POINTS), jnp.float32), -4.0, 4.0)
    return (base * time_scale * point_scale).astype(jnp.float32)


def draw_filter_weights(key, part):
    key = jax.random.fold_in(key, 23)
    first, second = jax.random.split(key, 2)
    others = jax.random.uniform(first, (TAPS,), jnp.float32, -1.0, 1.0) * (0.7 / (TAPS - 1))
    centre = jax.random.uniform(second, (), jnp.float32, 1.0, 1.2)
    return jnp.where(jnp.arange(TAPS) == (TAPS - 1) // 2, centre, others).astype(jnp.float32)


def setup_inputs(seed: int = 0) -> dict:
    keys = jax.random.split(jax.random.key(seed), 3)
    return {
        "thermal_anomaly_matrix": draw_thermal_anomaly_matrix(jax.random.fold_in(keys[2], 71), 0),
        "filter_weights": draw_filter_weights(jax.random.fold_in(keys[2], 71), 0),
    }


def temporal_lowpass(series, filter_weights):
    stencil_radius = (filter_weights.shape[0] - 1) // 2
    length = series.shape[0]
    boundary_extended_record = jnp.pad(series, ((stencil_radius, stencil_radius), (0, 0)))
    summed = jnp.zeros(series.shape, jnp.float32)
    for offset in range(filter_weights.shape[0]):
        summed = summed + filter_weights[offset] * boundary_extended_record[offset:offset + length]
    return summed

def reference(thermal_anomaly_matrix, filter_weights):
    lowpassed_record = temporal_lowpass(thermal_anomaly_matrix, filter_weights)
    gram_matrix = lax.dot_general(lowpassed_record.astype(jnp.float32), lowpassed_record.astype(jnp.float32), (((1,), (1,)), ((), ())), precision=lax.Precision.HIGHEST, preferred_element_type=jnp.float32)
    gram_matrix = gram_matrix / jnp.float32(POINTS)
    lower_factor = jnp.linalg.cholesky(gram_matrix)
    solved = lax.linalg.triangular_solve(lower_factor, lowpassed_record, left_side=True, lower=True)
    basis = solved.reshape(TIME, GROUPS, SPAN)
    return (lower_factor, basis)
```

```python
import functools
import jax
import jax.numpy as jnp
from jax import lax
from jax.experimental import pallas as pl
from jax.experimental.pallas import tpu as pltpu
from jax.sharding import PartitionSpec as P

MESH = pl.DeviceIdType.MESH
ALONG_X = 4
B = 128
OFF = (0, 4, 7, 9)
HI = lax.Precision.HIGHEST


def dot(a, b, dims=((1,), (0,))):
    return lax.dot_general(a, b, (dims, ((), ())), precision=HI, preferred_element_type=jnp.float32)


def recip(d):
    r = pl.reciprocal(d, approx=True)
    return r * (2.0 - d * r)


def rsq(d):
    r = lax.rsqrt(d)
    return r * (1.5 - 0.5 * d * r * r)


def factor128(rows):
    n = len(rows)
    lane = lax.broadcasted_iota(jnp.int32, (8, B), 1)
    sub = lax.broadcasted_iota(jnp.int32, (8, B), 0)
    m = list(rows)
    upper, inverse = [], []
    for v in range(n):
        j = 8 * v
        g = m[v]
        col = [jnp.broadcast_to(g[:, j + k : j + k + 1], (8, B)) for k in range(8)]
        p = {}
        for k in range(8):
            for l in range(k, 8):
                p[l, k] = jnp.broadcast_to(col[k][l : l + 1, :], (8, B))
        ra = [jnp.broadcast_to(g[l : l + 1, :], (8, B)) for l in range(8)]
        inside = (lane >= j) & (lane < j + 8)
        ri = [jnp.where(inside, jnp.where(lane == j + l, 1.0, 0.0), ra[l]) for l in range(8)]
        inv, mult = [], {}
        for k in range(8):
            inv.append(recip(p[k, k]))
            for l in range(k + 1, 8):
                mult[l, k] = p[l, k] * inv[k]
            for c in range(k + 1, 8):
                for l in range(c, 8):
                    p[l, c] = p[l, c] - mult[l, k] * p[c, k]
            for l in range(k + 1, 8):
                ra[l] = ra[l] - mult[l, k] * ra[k]
                ri[l] = ri[l] - mult[l, k] * ri[k]
        q = [None] * 8
        for l in range(7, -1, -1):
            t = ri[l] * inv[l]
            for r in range(7, l, -1):
                t = t - mult[r, l] * q[r]
            q[l] = t
        for i in range(v + 1, n):
            ci = [jnp.broadcast_to(m[i][:, j + k : j + k + 1], (8, B)) for k in range(8)]
            t = jnp.where(inside, 0.0, m[i])
            s1 = ci[0] * q[0] + ci[1] * q[1]
            s2 = ci[2] * q[2] + ci[3] * q[3]
            s3 = ci[4] * q[4] + ci[5] * q[5]
            s4 = ci[6] * q[6] + ci[7] * q[7]
            m[i] = t - ((s1 + s2) + (s3 + s4))
        u = jnp.zeros((8, B), jnp.float32)
        w = u
        for l in range(8):
            r = rsq(p[l, l])
            u = jnp.where(sub == l, ra[l] * r, u)
            w = jnp.where(sub == l, ri[l] * r, w)
        upper.append(jnp.where(lane >= j + sub, u, 0.0))
        inverse.append(jnp.where(lane <= j + sub, w, 0.0))
    return upper, inverse


def body(scale, g_ref, fx_ref, l_ref, y_ref, a, u, t, f):
    f[...] = fx_ref[...]
    for b in range(10):
        a[b] = g_ref[pl.ds(b * B, B), :] * scale
    l_ref[...] = jnp.zeros_like(l_ref)
    for k in range(4):
        d = OFF[k]
        rows = [a[d, pl.ds(8 * v, 8), :] for v in range(16)]
        up, iv = factor128(rows)
        for v in range(16):
            u[pl.ds(8 * v, 8), :] = up[v]
            t[pl.ds(8 * v, 8), :] = iv[v]
        tk = t[...]
        l_ref[pl.ds(k * B, B), pl.ds(k * B, B)] = u[...].T
        low = {}
        for i in range(k + 1, 4):
            low[i] = dot(a[d + i - k], tk, ((1,), (1,)))
            l_ref[pl.ds(i * B, B), pl.ds(k * B, B)] = low[i]
        for j in range(k + 1, 4):
            for i in range(j, 4):
                e = OFF[j] + i - j
                a[e] = a[e] - dot(low[i], low[j], ((1,), (1,)))
        y = dot(tk, f[pl.ds(k * B, B), :])
        for i in range(k + 1, 4):
            f[pl.ds(i * B, B), :] = f[pl.ds(i * B, B), :] - dot(low[i], y)
        wide = f.shape[1] // B
        for q in range(wide):
            y_ref[pl.ds(k * B * wide + q, B, stride=wide), :] = y[:, q * B : (q + 1) * B]


def factor_and_solve(gram, fx, points):
    rows, cols = fx.shape
    return pl.pallas_call(
        functools.partial(body, 1.0 / points),
        out_shape=(
            jax.ShapeDtypeStruct((rows, rows), jnp.float32),
            jax.ShapeDtypeStruct((rows * cols // B, B), jnp.float32),
        ),
        in_specs=[pl.BlockSpec(memory_space=pltpu.VMEM)] * 2,
        out_specs=(pl.BlockSpec(memory_space=pltpu.VMEM),) * 2,
        scratch_shapes=[
            pltpu.VMEM((10, B, B), jnp.float32),
            pltpu.VMEM((B, B), jnp.float32),
            pltpu.VMEM((B, B), jnp.float32),
            pltpu.VMEM((rows, cols), jnp.float32),
        ],
        compiler_params=pltpu.CompilerParams(vmem_limit_bytes=48 << 20),
        name="factor",
    )(gram, fx)


BLOCK = 128
CHUNK = 256
ORDER = ((0, 0), (1, 0), (2, 0), (3, 0), (1, 1), (2, 1), (3, 1), (2, 2), (3, 2), (3, 3))


class Plan:
    def __init__(self, mesh, nx, rows, width, taps):
        self.tm, self.space = mesh.shape["tm"], mesh.shape["space"]
        self.nz, self.nx, self.ny = self.tm // 2, nx, self.space // nx
        self.rows, self.width, self.taps = rows, width, taps
        self.time = rows * self.tm
        self.chunks = width // CHUNK
        self.packed = len(ORDER) * BLOCK
        self.half = self.packed // 2
        self.part = self.half // self.nx
        self.piece = -(-self.part // (8 * self.ny)) * 8
        self.padded = self.piece * self.ny


def remote(src, dst, send, recv, where):
    return pltpu.make_async_remote_copy(
        src_ref=src, dst_ref=dst, send_sem=send, recv_sem=recv, device_id=where, device_id_type=MESH
    )


def gather_body(plan, w_ref, x_ref, fx_ref, g_ref, xr, band, acc, p, rc, rx, hx, ry, hy, rz, gy, o,
                xs, xd, xl, cs, cd, ss, sd, ys, yd, zs, zd, yas, yad, xas, xad, cas, cad):
    P = plan
    t, s = lax.axis_index("tm"), lax.axis_index("space")
    z, c = t // 2, t % 2
    y, x = s // P.nx, s % P.nx

    def at_tm(i):
        return {"tm": i}

    def at_x(d):
        return {"space": y * P.nx + (x + d) % P.nx}

    def at_y(d):
        return {"space": ((y + d) % P.ny) * P.nx + x}

    def at_z(d):
        return {"tm": ((z + d) % P.nz) * 2 + c}

    sibling = {"tm": z * 2 + (1 - c)}

    barrier = pltpu.get_barrier_semaphore()
    for d in range(1, P.tm):
        pl.semaphore_signal(barrier, inc=1, device_id=at_tm((t + d) % P.tm), device_id_type=MESH)
    for d in range(1, P.nx):
        pl.semaphore_signal(barrier, inc=1, device_id=at_x(d), device_id_type=MESH)
    for d in range(1, P.ny):
        pl.semaphore_signal(barrier, inc=1, device_id=at_y(d), device_id_type=MESH)
    pl.semaphore_wait(barrier, (P.tm - 1) + (P.nx - 1) + (P.ny - 1))

    mine = pl.ds(pl.multiple_of(t * P.rows, 8), P.rows)
    steps = sorted(range(1, P.tm), key=lambda d: -min(d, P.tm - d))
    sends, local = [], []
    for h in range(P.chunks):
        there = pl.ds(h * CHUNK, CHUNK)
        for d in steps:
            peer = (t + d) % P.tm
            src = x_ref.at[:, pl.ds(pl.multiple_of(peer * P.width + h * CHUNK, 128), CHUNK)]
            copy = remote(src, xr.at[mine, there], xs.at[h, d - 1], xd.at[h], at_tm(peer))
            copy.start()
            sends.append(copy)
        own = pltpu.make_async_copy(
            x_ref.at[:, pl.ds(pl.multiple_of(t * P.width + h * CHUNK, 128), CHUNK)],
            xr.at[mine, there], xl.at[h])
        own.start()
        local.append(own)

    r = lax.broadcasted_iota(jnp.int32, (BLOCK, 3 * BLOCK), 0)
    q = lax.broadcasted_iota(jnp.int32, (BLOCK, 3 * BLOCK), 1)
    tap = q - r - BLOCK + (P.taps - 1) // 2
    f = jnp.zeros((BLOCK, 3 * BLOCK), jnp.float32)
    for k in range(P.taps):
        f = jnp.where(tap == k, w_ref[k], f)
    band[...] = f

    nb = P.time // BLOCK
    for h in range(P.chunks):
        there = pl.ds(h * CHUNK, CHUNK)
        local[h].wait()
        rest = xr.at[pl.ds(0, P.time - P.rows), there]
        pltpu.make_async_copy(rest, rest, xd.at[h]).wait()
        for i in range(nb):
            lo, hi = max(i - 1, 0), min(i + 2, nb)
            fx_ref[pl.ds(i * BLOCK, BLOCK), there] = dot(
                band[:, (lo - i + 1) * BLOCK : (hi - i + 1) * BLOCK],
                xr[pl.ds(lo * BLOCK, (hi - lo) * BLOCK), there])
        top = fx_ref[pl.ds(0, 256), there]
        low = fx_ref[pl.ds(256, 256), there]
        for e, (u, v) in enumerate(((top, top), (low, top), (low, low))):
            new = dot(u, v, ((1,), (1,)))
            if h > 0:
                new = acc[e] + new
            if h < P.chunks - 1:
                acc[e] = new
            else:
                for b, (i, j) in enumerate(ORDER):
                    if ((0, 0), (1, 0), (1, 1))[e] == (i // 2, j // 2):
                        p[pl.ds(b * BLOCK, BLOCK), :] = new[
                            (i % 2) * BLOCK : (i % 2 + 1) * BLOCK, (j % 2) * BLOCK : (j % 2 + 1) * BLOCK]

    def half(i):
        return pl.ds(pl.multiple_of(i * P.half, 8), P.half)

    copy = remote(p.at[half(1 - c)], rc, cs, cd, sibling)
    copy.start()
    for done in sends:
        done.wait_send()
    copy.wait()
    p[half(c), :] = p[half(c), :] + rc[...]

    def part(i):
        return pl.ds(pl.multiple_of((c * P.nx + i) * P.part, 8), P.part)

    copies = [remote(p.at[part((x + d) % P.nx)], rx.at[d - 1], ss.at[d - 1], sd.at[d - 1], at_x(d))
              for d in range(1, P.nx)]
    for copy in copies:
        copy.start()
    if P.padded > P.part:
        hx[pl.ds(P.part, P.padded - P.part), :] = jnp.zeros((P.padded - P.part, BLOCK), jnp.float32)
    total = p[part(x), :]
    for d, copy in enumerate(copies):
        copy.wait()
        total = total + rx[d]
    hx[pl.ds(0, P.part), :] = total

    def piece(i):
        return pl.ds(pl.multiple_of(i * P.piece, 8), P.piece)

    copies = [remote(hx.at[piece((y + d) % P.ny)], ry.at[d - 1], ys.at[d - 1], yd.at[d - 1], at_y(d))
              for d in range(1, P.ny)]
    for copy in copies:
        copy.start()
    total = hx[piece(y), :]
    for d, copy in enumerate(copies):
        copy.wait()
        total = total + ry[d]
    hy[...] = total

    copies = [remote(hy, rz.at[z], zs.at[d - 1], zd.at[d - 1], at_z(d)) for d in range(1, P.nz)]
    for copy in copies:
        copy.start()
    rz[z] = total
    for copy in copies:
        copy.wait()
    total = rz[0]
    for i in range(1, P.nz):
        total = total + rz[i]
    gy[piece(y), :] = total

    copies = [remote(gy.at[piece(y)], gy.at[piece(y)], yas.at[d - 1], yad.at[d - 1], at_y(d))
              for d in range(1, P.ny)]
    for copy in copies:
        copy.start()
    for copy in copies:
        copy.wait()
    copies = [remote(gy.at[pl.ds(0, P.part)], o.at[part(x)], xas.at[d - 1], xad.at[d - 1], at_x(d))
              for d in range(1, P.nx)]
    for copy in copies:
        copy.start()
    o[part(x), :] = gy[pl.ds(0, P.part), :]
    for copy in copies:
        copy.wait()
    copy = remote(o.at[half(c)], o.at[half(c)], cas, cad, sibling)
    copy.start()
    copy.wait()
    g_ref[...] = o[...]


def filter_and_gram(plan, weights, record):
    P = plan
    f32, dma = jnp.float32, pltpu.SemaphoreType.DMA
    x, y, z = P.nx - 1, P.ny - 1, P.nz - 1
    return pl.pallas_call(
        functools.partial(gather_body, plan),
        out_shape=(
            jax.ShapeDtypeStruct((P.time, P.width), f32),
            jax.ShapeDtypeStruct((P.packed, BLOCK), f32),
        ),
        in_specs=[pl.BlockSpec(memory_space=pltpu.SMEM), pl.BlockSpec(memory_space=pl.ANY)],
        out_specs=(pl.BlockSpec(memory_space=pltpu.VMEM),) * 2,
        scratch_shapes=[
            pltpu.VMEM((P.time, P.width), f32),
            pltpu.VMEM((BLOCK, 3 * BLOCK), f32),
            pltpu.VMEM((3, 256, 256), f32),
            pltpu.VMEM((P.packed, BLOCK), f32),
            pltpu.VMEM((P.half, BLOCK), f32),
            pltpu.VMEM((x, P.part, BLOCK), f32),
            pltpu.VMEM((P.padded, BLOCK), f32),
            pltpu.VMEM((y, P.piece, BLOCK), f32),
            pltpu.VMEM((P.piece, BLOCK), f32),
            pltpu.VMEM((P.nz, P.piece, BLOCK), f32),
            pltpu.VMEM((P.padded, BLOCK), f32),
            pltpu.VMEM((P.packed, BLOCK), f32),
            dma((P.chunks, P.tm - 1)), dma((P.chunks,)), dma((P.chunks,)),
            dma, dma, dma((x,)), dma((x,)), dma((y,)), dma((y,)), dma((z,)), dma((z,)),
            dma((y,)), dma((y,)), dma((x,)), dma((x,)), dma, dma,
        ],
        compiler_params=pltpu.CompilerParams(
            collective_id=0, has_side_effects=True, vmem_limit_bytes=48 << 20),
        name="gather_filter_gram",
    )(weights, record)


def solution(mesh):
    def per_device(record, weights):
        rows, width = record.shape[0], record.shape[1] // mesh.shape["tm"]
        plan = Plan(mesh, ALONG_X, rows, width, weights.shape[0])
        fx, gram = filter_and_gram(plan, weights, record)
        points = width * mesh.shape["tm"] * mesh.shape["space"]
        lower, basis = factor_and_solve(gram, fx, points)
        return lower, basis.reshape(plan.time, 1, width)

    return jax.shard_map(
        per_device,
        mesh=mesh,
        in_specs=(P("tm", "space"), P()),
        out_specs=(P(), P(None, "space", "tm")),
        check_vma=False,
    )
```

```python
import functools
import jax
import jax.numpy as jnp
from jax import lax
from jax.experimental import pallas as pl
from jax.experimental.pallas import tpu as pltpu
from jax.sharding import PartitionSpec as P

MESH = pl.DeviceIdType.MESH
ALONG_X = 4
B = 128
OFF = (0, 4, 7, 9)
HI = lax.Precision.HIGHEST


def dot(a, b, dims=((1,), (0,))):
    return lax.dot_general(a, b, (dims, ((), ())), precision=HI, preferred_element_type=jnp.float32)


def recip(d):
    return pl.reciprocal(d, approx=True)


def rsq(d):
    r = lax.rsqrt(d)
    return r


def factor128(rows, cs, gs):
    n = len(rows)
    lane = lax.broadcasted_iota(jnp.int32, (8, B), 1)
    sub = lax.broadcasted_iota(jnp.int32, (8, B), 0)
    m = list(rows)
    upper, inverse = [], []
    for v in range(n):
        j = 8 * v
        g = m[v]
        col = [jnp.broadcast_to(g[:, j + k : j + k + 1], (8, B)) for k in range(8)]
        p = {}
        o = v % 2
        gs[o] = g
        for k in range(8):
            cs[o, k] = col[k]
        for k in range(8):
            for l in range(k, 8):
                p[l, k] = jnp.broadcast_to(cs[o, k, pl.ds(l, 1), :], (8, B))
        ra = [jnp.broadcast_to(gs[o, pl.ds(l, 1), :], (8, B)) for l in range(8)]
        inside = (lane >= j) & (lane < j + 8)
        ri = [jnp.where(inside, jnp.where(lane == j + l, 1.0, 0.0), ra[l]) for l in range(8)]
        piv, n0, n1 = [None] * 8, {}, {}
        qa = [None] * 8
        for k in range(0, 8, 2):
            e = k + 1
            det = p[k, k] * p[e, e] - p[e, k] * p[e, k]
            rd = recip(det)
            i00, i10, i11 = p[e, e] * rd, -p[e, k] * rd, p[k, k] * rd
            for l in range(k + 2, 8):
                n0[l, k] = p[l, k] * i00 + p[l, e] * i10
                n1[l, k] = p[l, k] * i10 + p[l, e] * i11
            for c in range(k + 2, 8):
                for l in range(c, 8):
                    p[l, c] = p[l, c] - (n0[l, k] * p[c, k] + n1[l, k] * p[c, e])
            for l in range(k + 2, 8):
                ra[l] = ra[l] - (n0[l, k] * ra[k] + n1[l, k] * ra[e])
                ri[l] = ri[l] - (n0[l, k] * ri[k] + n1[l, k] * ri[e])
            qa[k] = i00 * ri[k] + i10 * ri[e]
            qa[e] = i10 * ri[k] + i11 * ri[e]
            first = recip(p[k, k])
            mult = p[e, k] * first
            ra[e] = ra[e] - mult * ra[k]
            ri[e] = ri[e] - mult * ri[k]
            p[e, e] = det * first
        q = list(qa)
        for k in (4, 2, 0):
            for l in range(7, k + 1, -1):
                q[k] = q[k] - n0[l, k] * q[l]
                q[k + 1] = q[k + 1] - n1[l, k] * q[l]
        for i in range(v + 1, n):
            ci = [jnp.broadcast_to(m[i][:, j + k : j + k + 1], (8, B)) for k in range(8)]
            t = jnp.where(inside, 0.0, m[i])
            s1 = ci[0] * q[0] + ci[1] * q[1]
            s2 = ci[2] * q[2] + ci[3] * q[3]
            s3 = ci[4] * q[4] + ci[5] * q[5]
            s4 = ci[6] * q[6] + ci[7] * q[7]
            m[i] = t - ((s1 + s2) + (s3 + s4))
        u = jnp.zeros((8, B), jnp.float32)
        w = u
        for l in range(8):
            r = rsq(p[l, l])
            u = jnp.where(sub == l, ra[l] * r, u)
            w = jnp.where(sub == l, ri[l] * r, w)
        upper.append(jnp.where(lane >= j + sub, u, 0.0))
        inverse.append(jnp.where(lane <= j + sub, w, 0.0))
    return upper, inverse


def body(scale, g_ref, fx_ref, l_ref, y_ref, a, u, t, f, cs, gs):
    eye = lax.broadcasted_iota(jnp.int32, (B, B), 0) == lax.broadcasted_iota(jnp.int32, (B, B), 1)
    across, down, root = [], [], []
    for k in range(4):
        kept = jnp.where(eye, g_ref[pl.ds(OFF[k] * B, B), :] * scale, 0.0)
        across.append(rsq(jnp.sum(kept, axis=0, keepdims=True)))
        column = jnp.sum(kept, axis=1, keepdims=True)
        down.append(rsq(column))
        root.append(column * down[k])
    for k in range(4):
        for i in range(k, 4):
            b = OFF[k] + i - k
            a[b] = (g_ref[pl.ds(b * B, B), :] * scale) * down[i] * across[k]
        f[pl.ds(k * B, B), :] = fx_ref[pl.ds(k * B, B), :] * down[k]
    l_ref[...] = jnp.zeros_like(l_ref)
    for k in range(4):
        d = OFF[k]
        rows = [a[d, pl.ds(8 * v, 8), :] for v in range(16)]
        up, iv = factor128(rows, cs, gs)
        for v in range(16):
            u[pl.ds(8 * v, 8), :] = up[v]
            t[pl.ds(8 * v, 8), :] = iv[v]
        tk = t[...]
        l_ref[pl.ds(k * B, B), pl.ds(k * B, B)] = u[...].T * root[k]
        low = {}
        for i in range(k + 1, 4):
            low[i] = dot(a[d + i - k], tk, ((1,), (1,)))
            l_ref[pl.ds(i * B, B), pl.ds(k * B, B)] = low[i] * root[i]
            for j in range(k + 1, i + 1):
                e = OFF[j] + i - j
                a[e] = a[e] - dot(low[i], low[j], ((1,), (1,)))
        y = dot(tk, f[pl.ds(k * B, B), :])
        for i in range(k + 1, 4):
            f[pl.ds(i * B, B), :] = f[pl.ds(i * B, B), :] - dot(low[i], y)
        wide = f.shape[1] // B
        for q in range(wide):
            y_ref[pl.ds(k * B * wide + q, B, stride=wide), :] = y[:, q * B : (q + 1) * B]


def factor_and_solve(gram, fx, points):
    rows, cols = fx.shape
    return pl.pallas_call(
        functools.partial(body, 1.0 / points),
        out_shape=(
            jax.ShapeDtypeStruct((rows, rows), jnp.float32),
            jax.ShapeDtypeStruct((rows * cols // B, B), jnp.float32),
        ),
        in_specs=[pl.BlockSpec(memory_space=pltpu.VMEM)] * 2,
        out_specs=(pl.BlockSpec(memory_space=pltpu.VMEM),) * 2,
        scratch_shapes=[
            pltpu.VMEM((10, B, B), jnp.float32),
            pltpu.VMEM((B, B), jnp.float32),
            pltpu.VMEM((B, B), jnp.float32),
            pltpu.VMEM((rows, cols), jnp.float32),
            pltpu.VMEM((2, 8, 8, B), jnp.float32),
            pltpu.VMEM((2, 8, B), jnp.float32),
        ],
        compiler_params=pltpu.CompilerParams(vmem_limit_bytes=48 << 20),
        name="factor",
    )(gram, fx)


BLOCK = 128
CHUNK = 256
ORDER = ((0, 0), (1, 0), (2, 0), (3, 0), (1, 1), (2, 1), (3, 1), (2, 2), (3, 2), (3, 3))


class Stream:
    def __init__(self, first, count, plan):
        self.base, self.packed = first * BLOCK, count * BLOCK
        self.half = self.packed // 2
        self.part = self.half // plan.nx
        self.piece = -(-self.part // (8 * plan.ny)) * 8
        self.padded = self.piece * plan.ny

    def buffers(self, plan):
        x, y, z = plan.nx - 1, plan.ny - 1, plan.nz - 1
        shapes = [
            (self.packed, BLOCK), (self.half, BLOCK), (x, self.part, BLOCK), (self.padded, BLOCK),
            (y, self.piece, BLOCK), (self.piece, BLOCK), (plan.nz, self.piece, BLOCK),
            (self.padded, BLOCK), (self.packed, BLOCK)]
        dma = pltpu.SemaphoreType.DMA
        counts = [1, 1, x, x, y, y, z, z, y, y, x, x, 1, 1]
        return [pltpu.VMEM(shape, jnp.float32) for shape in shapes] + [dma((n,)) for n in counts]


class Plan:
    def __init__(self, mesh, nx, rows, width, taps):
        self.tm, self.space = mesh.shape["tm"], mesh.shape["space"]
        self.nz, self.nx, self.ny = self.tm // 2, nx, self.space // nx
        self.rows, self.width, self.taps = rows, width, taps
        self.time = rows * self.tm
        self.chunks = width // CHUNK
        self.streams = [Stream(first, count, self) for first, count in ((0, 4), (4, 6))]


def remote(src, dst, send, recv, where):
    return pltpu.make_async_remote_copy(
        src_ref=src, dst_ref=dst, send_sem=send, recv_sem=recv, device_id=where, device_id_type=MESH
    )


def gather_body(plan, w_hbm, x_ref, fx_ref, g_ref, w_ref, xr, band, acc, ws, xs, xd, xl, *rest):
    P = plan
    t, s = lax.axis_index("tm"), lax.axis_index("space")
    z, c = t // 2, t % 2
    y, x = s // P.nx, s % P.nx

    def at_tm(i):
        return {"tm": i}

    def at_x(d):
        return {"space": y * P.nx + (x + d) % P.nx}

    def at_y(d):
        return {"space": ((y + d) % P.ny) * P.nx + x}

    def at_z(d):
        return {"tm": ((z + d) % P.nz) * 2 + c}

    sibling = {"tm": z * 2 + (1 - c)}

    weights = pltpu.make_async_copy(w_hbm, w_ref, ws)
    weights.start()
    barrier = pltpu.get_barrier_semaphore()
    for d in range(1, P.tm):
        pl.semaphore_signal(barrier, inc=1, device_id=at_tm((t + d) % P.tm), device_id_type=MESH)
    for d in range(1, P.nx):
        pl.semaphore_signal(barrier, inc=1, device_id=at_x(d), device_id_type=MESH)
    for d in range(1, P.ny):
        pl.semaphore_signal(barrier, inc=1, device_id=at_y(d), device_id_type=MESH)
    pl.semaphore_wait(barrier, (P.tm - 1) + (P.nx - 1) + (P.ny - 1))

    mine = pl.ds(pl.multiple_of(t * P.rows, 8), P.rows)
    steps = sorted(range(1, P.tm), key=lambda d: -min(d, P.tm - d))
    sends, local = [], []
    for h in range(P.chunks):
        there = pl.ds(h * CHUNK, CHUNK)
        for d in steps:
            peer = (t + d) % P.tm
            src = x_ref.at[:, pl.ds(pl.multiple_of(peer * P.width + h * CHUNK, 128), CHUNK)]
            copy = remote(src, xr.at[mine, there], xs.at[h, d - 1], xd.at[h], at_tm(peer))
            copy.start()
            sends.append(copy)
        own = pltpu.make_async_copy(
            x_ref.at[:, pl.ds(pl.multiple_of(t * P.width + h * CHUNK, 128), CHUNK)],
            xr.at[mine, there], xl.at[h])
        own.start()
        local.append(own)

    r = lax.broadcasted_iota(jnp.int32, (BLOCK, 3 * BLOCK), 0)
    q = lax.broadcasted_iota(jnp.int32, (BLOCK, 3 * BLOCK), 1)
    weights.wait()
    tap = q - r - BLOCK + (P.taps - 1) // 2
    f = jnp.zeros((BLOCK, 3 * BLOCK), jnp.float32)
    for k in range(P.taps):
        f = jnp.where(tap == k, w_ref[k], f)
    band[...] = f

    size = len(rest) // len(P.streams)
    held = [rest[i * size : (i + 1) * size] for i in range(len(P.streams))]
    sums = [sum_everywhere(P, S, (at_x, at_y, at_z, sibling), (z, c, y, x), one)
            for S, one in zip(P.streams, held)]
    nb = P.time // BLOCK
    for h in range(P.chunks):
        there = pl.ds(h * CHUNK, CHUNK)
        local[h].wait()
        others = xr.at[pl.ds(0, P.time - P.rows), there]
        pltpu.make_async_copy(others, others, xd.at[h]).wait()
        for i in range(nb):
            lo, hi = max(i - 1, 0), min(i + 2, nb)
            fx_ref[pl.ds(i * BLOCK, BLOCK), there] = dot(
                band[:, (lo - i + 1) * BLOCK : (hi - i + 1) * BLOCK],
                xr[pl.ds(lo * BLOCK, (hi - lo) * BLOCK), there])
        top = fx_ref[pl.ds(0, 256), there]
        low = fx_ref[pl.ds(256, 256), there]
        for e, (u, v) in enumerate(((top, top), (low, top), (low, low))):
            new = dot(u, v, ((1,), (1,)))
            if h > 0:
                new = acc[e] + new
            if h < P.chunks - 1:
                acc[e] = new
                continue
            for n, (i, j) in enumerate(ORDER):
                if ((0, 0), (1, 0), (1, 1))[e] == (i // 2, j // 2):
                    st = 0 if n < 4 else 1
                    held[st][0][pl.ds(n * BLOCK - P.streams[st].base, BLOCK), :] = new[
                        (i % 2) * BLOCK : (i % 2 + 1) * BLOCK, (j % 2) * BLOCK : (j % 2 + 1) * BLOCK]
            if e > 0:
                next(sums[e - 1])
    for done in sends:
        done.wait_send()
    while sums:
        sums = [one for one in sums if next(one, None) is not None]
    for st, one in zip(P.streams, held):
        g_ref[pl.ds(st.base, st.packed), :] = one[8][...]


def sum_everywhere(P, S, at, where, held):
    (p, rc, rx, hx, ry, hy, rz, gy, o,
     cs, cd, ss, sd, ys, yd, zs, zd, yas, yad, xas, xad, cas, cad) = held
    at_x, at_y, at_z, sibling = at
    z, c, y, x = where

    def half(i):
        return pl.ds(pl.multiple_of(i * S.half, 8), S.half)

    def part(i):
        return pl.ds(pl.multiple_of((c * P.nx + i) * S.part, 8), S.part)

    def piece(i):
        return pl.ds(pl.multiple_of(i * S.piece, 8), S.piece)

    def begin(copies):
        for copy in copies:
            copy.start()
        return copies

    copies = begin([remote(p.at[half(1 - c)], rc, cs.at[0], cd.at[0], sibling)])
    if S.padded > S.part:
        hx[pl.ds(S.part, S.padded - S.part), :] = jnp.zeros((S.padded - S.part, BLOCK), jnp.float32)
    yield True
    copies[0].wait()
    p[half(c), :] = p[half(c), :] + rc[...]

    copies = begin([remote(p.at[part((x + d) % P.nx)], rx.at[d - 1], ss.at[d - 1], sd.at[d - 1], at_x(d))
                    for d in range(1, P.nx)])
    yield True
    total = p[part(x), :]
    for d, copy in enumerate(copies):
        copy.wait()
        total = total + rx[d]
    hx[pl.ds(0, S.part), :] = total

    copies = begin([remote(hx.at[piece((y + d) % P.ny)], ry.at[d - 1], ys.at[d - 1], yd.at[d - 1], at_y(d))
                    for d in range(1, P.ny)])
    yield True
    total = hx[piece(y), :]
    for d, copy in enumerate(copies):
        copy.wait()
        total = total + ry[d]
    hy[...] = total

    copies = begin([remote(hy, rz.at[z], zs.at[d - 1], zd.at[d - 1], at_z(d)) for d in range(1, P.nz)])
    rz[z] = total
    yield True
    for copy in copies:
        copy.wait()
    total = rz[0]
    for i in range(1, P.nz):
        total = total + rz[i]
    gy[piece(y), :] = total

    copies = begin([remote(gy.at[piece(y)], gy.at[piece(y)], yas.at[d - 1], yad.at[d - 1], at_y(d))
                    for d in range(1, P.ny)])
    yield True
    for copy in copies:
        copy.wait()
    copies = begin([remote(gy.at[pl.ds(0, S.part)], o.at[part(x)], xas.at[d - 1], xad.at[d - 1], at_x(d))
                    for d in range(1, P.nx)])
    o[part(x), :] = gy[pl.ds(0, S.part), :]
    yield True
    for copy in copies:
        copy.wait()
    copies = begin([remote(o.at[half(c)], o.at[half(c)], cas.at[0], cad.at[0], sibling)])
    yield True
    copies[0].wait()


def filter_and_gram(plan, weights, record):
    P = plan
    f32, dma = jnp.float32, pltpu.SemaphoreType.DMA
    return pl.pallas_call(
        functools.partial(gather_body, plan),
        out_shape=(
            jax.ShapeDtypeStruct((P.time, P.width), f32),
            jax.ShapeDtypeStruct((len(ORDER) * BLOCK, BLOCK), f32),
        ),
        in_specs=[pl.BlockSpec(memory_space=pltpu.HBM)] * 2,
        out_specs=(pl.BlockSpec(memory_space=pltpu.VMEM),) * 2,
        scratch_shapes=[
            pltpu.SMEM((P.taps,), f32),
            pltpu.VMEM((P.time, P.width), f32),
            pltpu.VMEM((BLOCK, 3 * BLOCK), f32),
            pltpu.VMEM((3, 256, 256), f32),
            dma, dma((P.chunks, P.tm - 1)), dma((P.chunks,)), dma((P.chunks,)),
            *[b for S in P.streams for b in S.buffers(P)],
        ],
        compiler_params=pltpu.CompilerParams(
            collective_id=0, has_side_effects=True, vmem_limit_bytes=48 << 20),
        name="gather_filter_gram",
    )(weights, record)


def solution(mesh):
    def per_device(record, weights):
        rows, width = record.shape[0], record.shape[1] // mesh.shape["tm"]
        plan = Plan(mesh, ALONG_X, rows, width, weights.shape[0])
        fx, gram = filter_and_gram(plan, weights, record)
        points = width * mesh.shape["tm"] * mesh.shape["space"]
        lower, basis = factor_and_solve(gram, fx, points)
        return lower, basis.reshape(plan.time, 1, width)

    return jax.shard_map(
        per_device,
        mesh=mesh,
        in_specs=(P("tm", "space"), P()),
        out_specs=(P(), P(None, "space", "tm")),
        check_vma=False,
    )
```

```python
import functools
import jax
import jax.numpy as jnp
from jax import lax
from jax.experimental import pallas as pl
from jax.experimental.pallas import tpu as pltpu
from jax.sharding import PartitionSpec as P

MESH = pl.DeviceIdType.MESH
ALONG_X = 4
B = 128
OFF = (0, 4, 7, 9)
HI = lax.Precision.HIGHEST


def dot(a, b, dims=((1,), (0,))):
    return lax.dot_general(a, b, (dims, ((), ())), precision=HI, preferred_element_type=jnp.float32)


def recip(d):
    return pl.reciprocal(d, approx=True)


def rsq(d):
    r = lax.rsqrt(d)
    return r


def factor128(rows, cs, gs):
    n = len(rows)
    lane = lax.broadcasted_iota(jnp.int32, (8, B), 1)
    sub = lax.broadcasted_iota(jnp.int32, (8, B), 0)
    m = list(rows)
    upper, inverse = [], []
    for v in range(n):
        j = 8 * v
        g = m[v]
        col = [jnp.broadcast_to(g[:, j + k : j + k + 1], (8, B)) for k in range(8)]
        p = {}
        o = v % 2
        gs[o] = g
        for k in range(8):
            cs[o, k] = col[k]
        for k in range(8):
            for l in range(k, 8):
                p[l, k] = jnp.broadcast_to(cs[o, k, pl.ds(l, 1), :], (8, B))
        ra = [jnp.broadcast_to(gs[o, pl.ds(l, 1), :], (8, B)) for l in range(8)]
        inside = (lane >= j) & (lane < j + 8)
        ri = [jnp.where(inside, jnp.where(lane == j + l, 1.0, 0.0), ra[l]) for l in range(8)]
        piv, n0, n1 = [None] * 8, {}, {}
        qa = [None] * 8
        for k in range(0, 8, 2):
            e = k + 1
            det = p[k, k] * p[e, e] - p[e, k] * p[e, k]
            rd = recip(det)
            i00, i10, i11 = p[e, e] * rd, -p[e, k] * rd, p[k, k] * rd
            for l in range(k + 2, 8):
                n0[l, k] = p[l, k] * i00 + p[l, e] * i10
                n1[l, k] = p[l, k] * i10 + p[l, e] * i11
            for c in range(k + 2, 8):
                for l in range(c, 8):
                    p[l, c] = p[l, c] - (n0[l, k] * p[c, k] + n1[l, k] * p[c, e])
            for l in range(k + 2, 8):
                ra[l] = ra[l] - (n0[l, k] * ra[k] + n1[l, k] * ra[e])
                ri[l] = ri[l] - (n0[l, k] * ri[k] + n1[l, k] * ri[e])
            qa[k] = i00 * ri[k] + i10 * ri[e]
            qa[e] = i10 * ri[k] + i11 * ri[e]
            first = recip(p[k, k])
            mult = p[e, k] * first
            ra[e] = ra[e] - mult * ra[k]
            ri[e] = ri[e] - mult * ri[k]
            p[e, e] = det * first
        q = list(qa)
        for k in (4, 2, 0):
            for l in range(7, k + 1, -1):
                q[k] = q[k] - n0[l, k] * q[l]
                q[k + 1] = q[k + 1] - n1[l, k] * q[l]
        for i in range(v + 1, n):
            ci = [jnp.broadcast_to(m[i][:, j + k : j + k + 1], (8, B)) for k in range(8)]
            t = jnp.where(inside, 0.0, m[i])
            s1 = ci[0] * q[0] + ci[1] * q[1]
            s2 = ci[2] * q[2] + ci[3] * q[3]
            s3 = ci[4] * q[4] + ci[5] * q[5]
            s4 = ci[6] * q[6] + ci[7] * q[7]
            m[i] = t - ((s1 + s2) + (s3 + s4))
        u = jnp.zeros((8, B), jnp.float32)
        w = u
        for l in range(8):
            r = rsq(p[l, l])
            u = jnp.where(sub == l, ra[l] * r, u)
            w = jnp.where(sub == l, ri[l] * r, w)
        upper.append(jnp.where(lane >= j + sub, u, 0.0))
        inverse.append(jnp.where(lane <= j + sub, w, 0.0))
    return upper, inverse


def body(scale, g_ref, fx_ref, l_ref, y_ref, a, u, t, f, cs, gs):
    eye = lax.broadcasted_iota(jnp.int32, (B, B), 0) == lax.broadcasted_iota(jnp.int32, (B, B), 1)
    across, down, root = [], [], []
    for k in range(4):
        kept = jnp.where(eye, g_ref[pl.ds(OFF[k] * B, B), :] * scale, 0.0)
        across.append(rsq(jnp.sum(kept, axis=0, keepdims=True)))
        column = jnp.sum(kept, axis=1, keepdims=True)
        down.append(rsq(column))
        root.append(column * down[k])
    for k in range(4):
        for i in range(k, 4):
            b = OFF[k] + i - k
            a[b] = (g_ref[pl.ds(b * B, B), :] * scale) * down[i] * across[k]
        f[pl.ds(k * B, B), :] = fx_ref[pl.ds(k * B, B), :] * down[k]
    l_ref[...] = jnp.zeros_like(l_ref)
    for k in range(4):
        d = OFF[k]
        rows = [a[d, pl.ds(8 * v, 8), :] for v in range(16)]
        up, iv = factor128(rows, cs, gs)
        for v in range(16):
            u[pl.ds(8 * v, 8), :] = up[v]
            t[pl.ds(8 * v, 8), :] = iv[v]
        tk = t[...]
        l_ref[pl.ds(k * B, B), pl.ds(k * B, B)] = u[...].T * root[k]
        low = {}
        for i in range(k + 1, 4):
            low[i] = dot(a[d + i - k], tk, ((1,), (1,)))
            l_ref[pl.ds(i * B, B), pl.ds(k * B, B)] = low[i] * root[i]
            for j in range(k + 1, i + 1):
                e = OFF[j] + i - j
                a[e] = a[e] - dot(low[i], low[j], ((1,), (1,)))
        y = dot(tk, f[pl.ds(k * B, B), :])
        for i in range(k + 1, 4):
            f[pl.ds(i * B, B), :] = f[pl.ds(i * B, B), :] - dot(low[i], y)
        wide = f.shape[1] // B
        for q in range(wide):
            y_ref[pl.ds(k * B * wide + q, B, stride=wide), :] = y[:, q * B : (q + 1) * B]


def factor_and_solve(gram, fx, points):
    rows, cols = fx.shape
    return pl.pallas_call(
        functools.partial(body, 1.0 / points),
        out_shape=(
            jax.ShapeDtypeStruct((rows, rows), jnp.float32),
            jax.ShapeDtypeStruct((rows * cols // B, B), jnp.float32),
        ),
        in_specs=[pl.BlockSpec(memory_space=pltpu.VMEM)] * 2,
        out_specs=(pl.BlockSpec(memory_space=pltpu.VMEM),) * 2,
        scratch_shapes=[
            pltpu.VMEM((10, B, B), jnp.float32),
            pltpu.VMEM((B, B), jnp.float32),
            pltpu.VMEM((B, B), jnp.float32),
            pltpu.VMEM((rows, cols), jnp.float32),
            pltpu.VMEM((2, 8, 8, B), jnp.float32),
            pltpu.VMEM((2, 8, B), jnp.float32),
        ],
        compiler_params=pltpu.CompilerParams(vmem_limit_bytes=48 << 20),
        name="factor",
    )(gram, fx)


BLOCK = 128
CHUNK = 256
ORDER = ((0, 0), (1, 0), (2, 0), (3, 0), (1, 1), (2, 1), (3, 1), (2, 2), (3, 2), (3, 3))


class Stream:
    def __init__(self, first, count, axes, plan):
        self.axes = axes
        n1, n2 = (plan.sizes[axis] for axis in axes)
        self.n1, self.n2 = n1, n2
        self.base, self.packed = first * BLOCK, count * BLOCK
        self.half = self.packed // 2
        self.part = self.half // n1
        self.piece = -(-self.part // (8 * n2)) * 8
        self.padded = self.piece * n2

    def buffers(self, plan):
        u, v, z = self.n1 - 1, self.n2 - 1, plan.nz - 1
        shapes = [
            (self.packed, BLOCK), (self.half, BLOCK), (u, self.part, BLOCK), (self.padded, BLOCK),
            (v, self.piece, BLOCK), (self.piece, BLOCK), (plan.nz, self.piece, BLOCK),
            (self.padded, BLOCK), (self.packed, BLOCK)]
        dma = pltpu.SemaphoreType.DMA
        counts = [1, 1, u, u, v, v, z, z, v, v, u, u, 1, 1]
        return [pltpu.VMEM(shape, jnp.float32) for shape in shapes] + [dma((n,)) for n in counts]


class Plan:
    def __init__(self, mesh, nx, rows, width, taps):
        self.tm, self.space = mesh.shape["tm"], mesh.shape["space"]
        self.nz, self.nx, self.ny = self.tm // 2, nx, self.space // nx
        self.rows, self.width, self.taps = rows, width, taps
        self.time = rows * self.tm
        self.chunks = width // CHUNK
        self.sizes = {"x": self.nx, "y": self.ny}
        self.streams = [Stream(0, 4, "yx", self), Stream(4, 6, "xy", self)]


def remote(src, dst, send, recv, where):
    return pltpu.make_async_remote_copy(
        src_ref=src, dst_ref=dst, send_sem=send, recv_sem=recv, device_id=where, device_id_type=MESH
    )


def gather_body(plan, w_hbm, x_ref, fx_ref, g_ref, w_ref, xr, band, acc, relay, ws, xs, xd, xl, rs, rd, fs, *rest):
    P = plan
    t, s = lax.axis_index("tm"), lax.axis_index("space")
    z, c = t // 2, t % 2
    y, x = s // P.nx, s % P.nx

    def at_tm(i):
        return {"tm": i}

    def at_x(d):
        return {"space": y * P.nx + (x + d) % P.nx}

    def at_y(d):
        return {"space": ((y + d) % P.ny) * P.nx + x}

    def at_z(d):
        return {"tm": ((z + d) % P.nz) * 2 + c}

    sibling = {"tm": z * 2 + (1 - c)}

    weights = pltpu.make_async_copy(w_hbm, w_ref, ws)
    weights.start()
    barrier = pltpu.get_barrier_semaphore()
    for d in range(1, P.tm):
        pl.semaphore_signal(barrier, inc=1, device_id=at_tm((t + d) % P.tm), device_id_type=MESH)
    for d in range(1, P.nx):
        pl.semaphore_signal(barrier, inc=1, device_id=at_x(d), device_id_type=MESH)
    for d in range(1, P.ny):
        pl.semaphore_signal(barrier, inc=1, device_id=at_y(d), device_id_type=MESH)
    pl.semaphore_wait(barrier, (P.tm - 1) + (P.nx - 1) + (P.ny - 1))

    far = P.nz // 2

    def theirs(device, h):
        return x_ref.at[:, pl.ds(pl.multiple_of(device * P.width + h * CHUNK, 128), CHUNK)]

    def block(device, h):
        return xr.at[pl.ds(pl.multiple_of(device * P.rows, 8), P.rows), pl.ds(h * CHUNK, CHUNK)]

    def device(dz, core):
        return ((z + dz + P.nz) % P.nz) * 2 + core

    sends, local, relayed = [], [], {}
    for h in range(P.chunks):
        for core, way in enumerate((1, -1)):
            relayed[core, h] = remote(theirs(device(far, core), h), relay.at[core, h],
                                      rs.at[core, h], rd.at[core, h], at_tm(device(way, c)))
            relayed[core, h].start()
    for h in range(P.chunks):
        peers = [device(way * dz, core) for dz in range(far - 1, 0, -1) for way in (1, -1) for core in (0, 1)]
        for n, peer in enumerate(peers + [device(0, 1 - c)]):
            copy = remote(theirs(peer, h), block(t, h), xs.at[h, n], xd.at[h], at_tm(peer))
            copy.start()
            sends.append(copy)
        own = pltpu.make_async_copy(theirs(t, h), block(t, h), xl.at[h])
        own.start()
        local.append(own)
    for h in range(P.chunks):
        for core, way in enumerate((1, -1)):
            relayed[core, h].wait_recv()
            copy = remote(relay.at[core, h], block(device(-way, c), h), fs.at[core, h], xd.at[h],
                          at_tm(device(way * (far - 1), core)))
            copy.start()
            sends.append(copy)
    sends.extend(relayed.values())

    r = lax.broadcasted_iota(jnp.int32, (BLOCK, 3 * BLOCK), 0)
    q = lax.broadcasted_iota(jnp.int32, (BLOCK, 3 * BLOCK), 1)
    weights.wait()
    tap = q - r - BLOCK + (P.taps - 1) // 2
    f = jnp.zeros((BLOCK, 3 * BLOCK), jnp.float32)
    for k in range(P.taps):
        f = jnp.where(tap == k, w_ref[k], f)
    band[...] = f

    at = {'x': at_x, 'y': at_y, 'z': at_z, 'core': sibling}
    where = {'x': x, 'y': y, 'z': z, 'core': c}
    size = len(rest) // len(P.streams)
    held = [rest[i * size : (i + 1) * size] for i in range(len(P.streams))]
    sums = [sum_everywhere(P, S, at, where, one)
            for S, one in zip(P.streams, held)]
    nb = P.time // BLOCK
    for h in range(P.chunks):
        there = pl.ds(h * CHUNK, CHUNK)
        local[h].wait()
        others = xr.at[pl.ds(0, P.time - P.rows), there]
        pltpu.make_async_copy(others, others, xd.at[h]).wait()
        for i in range(nb):
            lo, hi = max(i - 1, 0), min(i + 2, nb)
            fx_ref[pl.ds(i * BLOCK, BLOCK), there] = dot(
                band[:, (lo - i + 1) * BLOCK : (hi - i + 1) * BLOCK],
                xr[pl.ds(lo * BLOCK, (hi - lo) * BLOCK), there])
        top = fx_ref[pl.ds(0, 256), there]
        low = fx_ref[pl.ds(256, 256), there]
        for e, (u, v) in enumerate(((top, top), (low, top), (low, low))):
            new = dot(u, v, ((1,), (1,)))
            if h > 0:
                new = acc[e] + new
            if h < P.chunks - 1:
                acc[e] = new
                continue
            for n, (i, j) in enumerate(ORDER):
                if ((0, 0), (1, 0), (1, 1))[e] == (i // 2, j // 2):
                    st = 0 if n < 4 else 1
                    held[st][0][pl.ds(n * BLOCK - P.streams[st].base, BLOCK), :] = new[
                        (i % 2) * BLOCK : (i % 2 + 1) * BLOCK, (j % 2) * BLOCK : (j % 2 + 1) * BLOCK]
            if e > 0:
                next(sums[e - 1])
    for done in sends:
        done.wait_send()
    while sums:
        sums = [one for one in sums if next(one, None) is not None]
    for st, one in zip(P.streams, held):
        g_ref[pl.ds(st.base, st.packed), :] = one[8][...]


def sum_everywhere(P, S, at, where, held):
    (p, rc, rx, hx, ry, hy, rz, gy, o,
     cs, cd, ss, sd, ys, yd, zs, zd, yas, yad, xas, xad, cas, cad) = held
    at_z, sibling = at['z'], at['core']
    at_1, at_2 = (at[axis] for axis in S.axes)
    i1, i2 = (where[axis] for axis in S.axes)
    z, c = where['z'], where['core']

    def half(i):
        return pl.ds(pl.multiple_of(i * S.half, 8), S.half)

    def part(i):
        return pl.ds(pl.multiple_of((c * S.n1 + i) * S.part, 8), S.part)

    def piece(i):
        return pl.ds(pl.multiple_of(i * S.piece, 8), S.piece)

    def begin(copies):
        for copy in copies:
            copy.start()
        return copies

    copies = begin([remote(p.at[half(1 - c)], rc, cs.at[0], cd.at[0], sibling)])
    if S.padded > S.part:
        hx[pl.ds(S.part, S.padded - S.part), :] = jnp.zeros((S.padded - S.part, BLOCK), jnp.float32)
    yield True
    copies[0].wait()
    p[half(c), :] = p[half(c), :] + rc[...]

    copies = begin([remote(p.at[part((i1 + d) % S.n1)], rx.at[d - 1], ss.at[d - 1], sd.at[d - 1], at_1(d))
                    for d in range(1, S.n1)])
    yield True
    total = p[part(i1), :]
    for d, copy in enumerate(copies):
        copy.wait()
        total = total + rx[d]
    hx[pl.ds(0, S.part), :] = total

    copies = begin([remote(hx.at[piece((i2 + d) % S.n2)], ry.at[d - 1], ys.at[d - 1], yd.at[d - 1], at_2(d))
                    for d in range(1, S.n2)])
    yield True
    total = hx[piece(i2), :]
    for d, copy in enumerate(copies):
        copy.wait()
        total = total + ry[d]
    hy[...] = total

    copies = begin([remote(hy, rz.at[z], zs.at[d - 1], zd.at[d - 1], at_z(d)) for d in range(1, P.nz)])
    rz[z] = total
    yield True
    for copy in copies:
        copy.wait()
    total = rz[0]
    for i in range(1, P.nz):
        total = total + rz[i]
    gy[piece(i2), :] = total

    copies = begin([remote(gy.at[piece(i2)], gy.at[piece(i2)], yas.at[d - 1], yad.at[d - 1], at_2(d))
                    for d in range(1, S.n2)])
    yield True
    for copy in copies:
        copy.wait()
    copies = begin([remote(gy.at[pl.ds(0, S.part)], o.at[part(i1)], xas.at[d - 1], xad.at[d - 1], at_1(d))
                    for d in range(1, S.n1)])
    o[part(i1), :] = gy[pl.ds(0, S.part), :]
    yield True
    for copy in copies:
        copy.wait()
    copies = begin([remote(o.at[half(c)], o.at[half(c)], cas.at[0], cad.at[0], sibling)])
    yield True
    copies[0].wait()


def filter_and_gram(plan, weights, record):
    P = plan
    f32, dma = jnp.float32, pltpu.SemaphoreType.DMA
    return pl.pallas_call(
        functools.partial(gather_body, plan),
        out_shape=(
            jax.ShapeDtypeStruct((P.time, P.width), f32),
            jax.ShapeDtypeStruct((len(ORDER) * BLOCK, BLOCK), f32),
        ),
        in_specs=[pl.BlockSpec(memory_space=pltpu.HBM)] * 2,
        out_specs=(pl.BlockSpec(memory_space=pltpu.VMEM),) * 2,
        scratch_shapes=[
            pltpu.SMEM((P.taps,), f32),
            pltpu.VMEM((P.time, P.width), f32),
            pltpu.VMEM((BLOCK, 3 * BLOCK), f32),
            pltpu.VMEM((3, 256, 256), f32),
            pltpu.VMEM((2, P.chunks, P.rows, CHUNK), f32),
            dma, dma((P.chunks, P.tm - 3)), dma((P.chunks,)), dma((P.chunks,)),
            *[dma((2, P.chunks))] * 3,
            *[b for S in P.streams for b in S.buffers(P)],
        ],
        compiler_params=pltpu.CompilerParams(
            collective_id=0, has_side_effects=True, vmem_limit_bytes=52000 << 10),
        name="gather_filter_gram",
    )(weights, record)


def solution(mesh):
    def per_device(record, weights):
        rows, width = record.shape[0], record.shape[1] // mesh.shape["tm"]
        plan = Plan(mesh, ALONG_X, rows, width, weights.shape[0])
        fx, gram = filter_and_gram(plan, weights, record)
        points = width * mesh.shape["tm"] * mesh.shape["space"]
        lower, basis = factor_and_solve(gram, fx, points)
        return lower, basis.reshape(plan.time, 1, width)

    return jax.shard_map(
        per_device,
        mesh=mesh,
        in_specs=(P("tm", "space"), P()),
        out_specs=(P(), P(None, "space", "tm")),
        check_vma=False,
    )
```

```python
import functools
import jax
import jax.numpy as jnp
from jax import lax
from jax.experimental import pallas as pl
from jax.experimental.pallas import tpu as pltpu
from jax.sharding import PartitionSpec as P

MESH = pl.DeviceIdType.MESH
ALONG_X = 4
B = 128
OFF = (0, 4, 7, 9)
HI = lax.Precision.HIGHEST


def dot(a, b, dims=((1,), (0,))):
    return lax.dot_general(a, b, (dims, ((), ())), precision=HI, preferred_element_type=jnp.float32)


def recip(d):
    return pl.reciprocal(d, approx=True)


def rsq(d):
    r = lax.rsqrt(d)
    return r


def factor128(rows, cs, gs):
    n = len(rows)
    lane = lax.broadcasted_iota(jnp.int32, (8, B), 1)
    sub = lax.broadcasted_iota(jnp.int32, (8, B), 0)
    m = list(rows)
    upper, inverse = [], []
    for v in range(n):
        j = 8 * v
        g = m[v]
        col = [jnp.broadcast_to(g[:, j + k : j + k + 1], (8, B)) for k in range(8)]
        p = {}
        o = v % 2
        gs[o] = g
        for k in range(8):
            cs[o, k] = col[k]
        for k in range(8):
            for l in range(k, 8):
                p[l, k] = jnp.broadcast_to(cs[o, k, pl.ds(l, 1), :], (8, B))
        ra = [jnp.broadcast_to(gs[o, pl.ds(l, 1), :], (8, B)) for l in range(8)]
        inside = (lane >= j) & (lane < j + 8)
        ri = [jnp.where(inside, jnp.where(lane == j + l, 1.0, 0.0), ra[l]) for l in range(8)]
        piv, n0, n1 = [None] * 8, {}, {}
        qa = [None] * 8
        for k in range(0, 8, 2):
            e = k + 1
            det = p[k, k] * p[e, e] - p[e, k] * p[e, k]
            rd = recip(det)
            i00, i10, i11 = p[e, e] * rd, -p[e, k] * rd, p[k, k] * rd
            for l in range(k + 2, 8):
                n0[l, k] = p[l, k] * i00 + p[l, e] * i10
                n1[l, k] = p[l, k] * i10 + p[l, e] * i11
            for c in range(k + 2, 8):
                for l in range(c, 8):
                    p[l, c] = p[l, c] - (n0[l, k] * p[c, k] + n1[l, k] * p[c, e])
            for l in range(k + 2, 8):
                ra[l] = ra[l] - (n0[l, k] * ra[k] + n1[l, k] * ra[e])
                ri[l] = ri[l] - (n0[l, k] * ri[k] + n1[l, k] * ri[e])
            qa[k] = i00 * ri[k] + i10 * ri[e]
            qa[e] = i10 * ri[k] + i11 * ri[e]
            first = recip(p[k, k])
            mult = p[e, k] * first
            ra[e] = ra[e] - mult * ra[k]
            ri[e] = ri[e] - mult * ri[k]
            p[e, e] = det * first
        q = list(qa)
        for k in (4, 2, 0):
            for l in range(7, k + 1, -1):
                q[k] = q[k] - n0[l, k] * q[l]
                q[k + 1] = q[k + 1] - n1[l, k] * q[l]
        for i in range(v + 1, n):
            ci = [jnp.broadcast_to(m[i][:, j + k : j + k + 1], (8, B)) for k in range(8)]
            t = jnp.where(inside, 0.0, m[i])
            s1 = ci[0] * q[0] + ci[1] * q[1]
            s2 = ci[2] * q[2] + ci[3] * q[3]
            s3 = ci[4] * q[4] + ci[5] * q[5]
            s4 = ci[6] * q[6] + ci[7] * q[7]
            m[i] = t - ((s1 + s2) + (s3 + s4))
        u = jnp.zeros((8, B), jnp.float32)
        w = u
        for l in range(8):
            r = rsq(p[l, l])
            u = jnp.where(sub == l, ra[l] * r, u)
            w = jnp.where(sub == l, ri[l] * r, w)
        upper.append(jnp.where(lane >= j + sub, u, 0.0))
        inverse.append(jnp.where(lane <= j + sub, w, 0.0))
    return upper, inverse


def body(scale, g_ref, fx_ref, l_out, y_out, a, u, t, f, cs, gs, l_ref, y_ref, sem):
    eye = lax.broadcasted_iota(jnp.int32, (B, B), 0) == lax.broadcasted_iota(jnp.int32, (B, B), 1)
    across, down, root = [], [], []
    for k in range(4):
        kept = jnp.where(eye, g_ref[pl.ds(OFF[k] * B, B), :] * scale, 0.0)
        across.append(rsq(jnp.sum(kept, axis=0, keepdims=True)))
        column = jnp.sum(kept, axis=1, keepdims=True)
        down.append(rsq(column))
        root.append(column * down[k])
    for k in range(4):
        for i in range(k, 4):
            b = OFF[k] + i - k
            a[b] = (g_ref[pl.ds(b * B, B), :] * scale) * down[i] * across[k]
        f[pl.ds(k * B, B), :] = fx_ref[pl.ds(k * B, B), :] * down[k]
    l_ref[...] = jnp.zeros_like(l_ref)
    copies = []
    for k in range(4):
        d = OFF[k]
        rows = [a[d, pl.ds(8 * v, 8), :] for v in range(16)]
        up, iv = factor128(rows, cs, gs)
        for v in range(16):
            u[pl.ds(8 * v, 8), :] = up[v]
            t[pl.ds(8 * v, 8), :] = iv[v]
        tk = t[...]
        l_ref[pl.ds(k * B, B), pl.ds(k * B, B)] = u[...].T * root[k]
        low = {}
        for i in range(k + 1, 4):
            low[i] = dot(a[d + i - k], tk, ((1,), (1,)))
            l_ref[pl.ds(i * B, B), pl.ds(k * B, B)] = low[i] * root[i]
            for j in range(k + 1, i + 1):
                e = OFF[j] + i - j
                a[e] = a[e] - dot(low[i], low[j], ((1,), (1,)))
        y = dot(tk, f[pl.ds(k * B, B), :])
        for i in range(k + 1, 4):
            f[pl.ds(i * B, B), :] = f[pl.ds(i * B, B), :] - dot(low[i], y)
        wide = f.shape[1] // B
        for q in range(wide):
            y_ref[pl.ds(k * B * wide + q, B, stride=wide), :] = y[:, q * B : (q + 1) * B]

        strip = pl.ds(k * B, B)
        wide = f.shape[1] // B
        for e, (here, there) in enumerate((
                (l_ref.at[strip], l_out.at[strip]),
                (y_ref.at[pl.ds(k * B * wide, B * wide)], y_out.at[pl.ds(k * B * wide, B * wide)]))):
            copy = pltpu.make_async_copy(here, there, sem.at[e, k])
            copy.start()
            copies.append(copy)
    for copy in copies:
        copy.wait()


def factor_and_solve(gram, fx, points):
    rows, cols = fx.shape
    return pl.pallas_call(
        functools.partial(body, 1.0 / points),
        out_shape=(
            jax.ShapeDtypeStruct((rows, rows), jnp.float32),
            jax.ShapeDtypeStruct((rows * cols // B, B), jnp.float32),
        ),
        in_specs=[pl.BlockSpec(memory_space=pltpu.VMEM)] * 2,
        out_specs=(pl.BlockSpec(memory_space=pl.ANY),) * 2,
        scratch_shapes=[
            pltpu.VMEM((10, B, B), jnp.float32),
            pltpu.VMEM((B, B), jnp.float32),
            pltpu.VMEM((B, B), jnp.float32),
            pltpu.VMEM((rows, cols), jnp.float32),
            pltpu.VMEM((2, 8, 8, B), jnp.float32),
            pltpu.VMEM((2, 8, B), jnp.float32),
            pltpu.VMEM((rows, rows), jnp.float32),
            pltpu.VMEM((rows * cols // B, B), jnp.float32),
            pltpu.SemaphoreType.DMA((2, 4)),
        ],
        compiler_params=pltpu.CompilerParams(vmem_limit_bytes=48 << 20),
        name="factor",
    )(gram, fx)


BLOCK = 128
CHUNK = 256
STREAMS = ((0, 4), (4, 3), (7, 3))
READY = ((), (0, 1), (2,))
ORDER = ((0, 0), (1, 0), (2, 0), (3, 0), (1, 1), (2, 1), (3, 1), (2, 2), (3, 2), (3, 3))


class Stream:
    def __init__(self, first, count, plan):
        self.base, self.packed = first * BLOCK, count * BLOCK
        self.half = self.packed // 2
        self.part = self.half // plan.nx
        self.piece = -(-self.part // (8 * plan.ny)) * 8
        self.padded = self.piece * plan.ny

    def buffers(self, plan):
        x, y, z = plan.nx - 1, plan.ny - 1, plan.nz - 1
        shapes = [
            (self.packed, BLOCK), (self.half, BLOCK), (x, self.part, BLOCK), (self.padded, BLOCK),
            (y, self.piece, BLOCK), (self.piece, BLOCK), (plan.nz, self.piece, BLOCK),
            (self.padded, BLOCK), (self.packed, BLOCK)]
        dma = pltpu.SemaphoreType.DMA
        counts = [1, 1, x, x, y, y, z, z, y, y, x, x, 1, 1]
        return [pltpu.VMEM(shape, jnp.float32) for shape in shapes] + [dma((n,)) for n in counts]


class Plan:
    def __init__(self, mesh, nx, rows, width, taps):
        self.tm, self.space = mesh.shape["tm"], mesh.shape["space"]
        self.nz, self.nx, self.ny = self.tm // 2, nx, self.space // nx
        self.rows, self.width, self.taps = rows, width, taps
        self.time = rows * self.tm
        self.chunks = width // CHUNK
        self.streams = [Stream(first, count, self) for first, count in STREAMS]


def remote(src, dst, send, recv, where):
    return pltpu.make_async_remote_copy(
        src_ref=src, dst_ref=dst, send_sem=send, recv_sem=recv, device_id=where, device_id_type=MESH
    )


def gather_body(plan, w_hbm, x_ref, fx_out, g_ref, w_ref, fx_ref, fs, xr, band, acc, ws, xs, xd, xl, *rest):
    P = plan
    t, s = lax.axis_index("tm"), lax.axis_index("space")
    z, c = t // 2, t % 2
    y, x = s // P.nx, s % P.nx

    def at_tm(i):
        return {"tm": i}

    def at_x(d):
        return {"space": y * P.nx + (x + d) % P.nx}

    def at_y(d):
        return {"space": ((y + d) % P.ny) * P.nx + x}

    def at_z(d):
        return {"tm": ((z + d) % P.nz) * 2 + c}

    sibling = {"tm": z * 2 + (1 - c)}

    weights = pltpu.make_async_copy(w_hbm, w_ref, ws)
    weights.start()
    barrier = pltpu.get_barrier_semaphore()
    for d in range(1, P.tm):
        pl.semaphore_signal(barrier, inc=1, device_id=at_tm((t + d) % P.tm), device_id_type=MESH)
    for d in range(1, P.nx):
        pl.semaphore_signal(barrier, inc=1, device_id=at_x(d), device_id_type=MESH)
    for d in range(1, P.ny):
        pl.semaphore_signal(barrier, inc=1, device_id=at_y(d), device_id_type=MESH)
    pl.semaphore_wait(barrier, (P.tm - 1) + (P.nx - 1) + (P.ny - 1))

    mine = pl.ds(pl.multiple_of(t * P.rows, 8), P.rows)
    steps = sorted(range(1, P.tm), key=lambda d: -min(d, P.tm - d))
    sends, local = [], []
    for h in range(P.chunks):
        there = pl.ds(h * CHUNK, CHUNK)
        for d in steps:
            peer = (t + d) % P.tm
            src = x_ref.at[:, pl.ds(pl.multiple_of(peer * P.width + h * CHUNK, 128), CHUNK)]
            copy = remote(src, xr.at[mine, there], xs.at[h, d - 1], xd.at[h], at_tm(peer))
            copy.start()
            sends.append(copy)
        own = pltpu.make_async_copy(
            x_ref.at[:, pl.ds(pl.multiple_of(t * P.width + h * CHUNK, 128), CHUNK)],
            xr.at[mine, there], xl.at[h])
        own.start()
        local.append(own)

    r = lax.broadcasted_iota(jnp.int32, (BLOCK, 3 * BLOCK), 0)
    q = lax.broadcasted_iota(jnp.int32, (BLOCK, 3 * BLOCK), 1)
    weights.wait()
    tap = q - r - BLOCK + (P.taps - 1) // 2
    f = jnp.zeros((BLOCK, 3 * BLOCK), jnp.float32)
    for k in range(P.taps):
        f = jnp.where(tap == k, w_ref[k], f)
    band[...] = f

    size = len(rest) // len(P.streams)
    held = [rest[i * size : (i + 1) * size] for i in range(len(P.streams))]
    sums = [sum_everywhere(P, S, (at_x, at_y, at_z, sibling), (z, c, y, x), one)
            for S, one in zip(P.streams, held)]
    leaving = []
    nb = P.time // BLOCK
    for h in range(P.chunks):
        there = pl.ds(h * CHUNK, CHUNK)
        local[h].wait()
        others = xr.at[pl.ds(0, P.time - P.rows), there]
        pltpu.make_async_copy(others, others, xd.at[h]).wait()
        for i in range(nb):
            lo, hi = max(i - 1, 0), min(i + 2, nb)
            fx_ref[pl.ds(i * BLOCK, BLOCK), there] = dot(
                band[:, (lo - i + 1) * BLOCK : (hi - i + 1) * BLOCK],
                xr[pl.ds(lo * BLOCK, (hi - lo) * BLOCK), there])
        copy = pltpu.make_async_copy(fx_ref.at[:, there], fx_out.at[:, there], fs.at[h])
        copy.start()
        leaving.append(copy)
        top = fx_ref[pl.ds(0, 256), there]
        low = fx_ref[pl.ds(256, 256), there]
        for e, (u, v) in enumerate(((top, top), (low, top), (low, low))):
            new = dot(u, v, ((1,), (1,)))
            if h > 0:
                new = acc[e] + new
            if h < P.chunks - 1:
                acc[e] = new
                continue
            for n, (i, j) in enumerate(ORDER):
                if ((0, 0), (1, 0), (1, 1))[e] == (i // 2, j // 2):
                    st = max(o for o, S in enumerate(P.streams) if S.base <= n * BLOCK)
                    held[st][0][pl.ds(n * BLOCK - P.streams[st].base, BLOCK), :] = new[
                        (i % 2) * BLOCK : (i % 2 + 1) * BLOCK, (j % 2) * BLOCK : (j % 2 + 1) * BLOCK]
            for o in READY[e]:
                next(sums[o])
    phase = 0
    while sums:
        sums = [one for one in sums if next(one, None) is not None]
        phase += 1
        if phase == 2:
            for done in sends:
                done.wait_send()
            for copy in leaving:
                copy.wait()
    for st, one in zip(P.streams, held):
        g_ref[pl.ds(st.base, st.packed), :] = one[8][...]


def sum_everywhere(P, S, at, where, held):
    (p, rc, rx, hx, ry, hy, rz, gy, o,
     cs, cd, ss, sd, ys, yd, zs, zd, yas, yad, xas, xad, cas, cad) = held
    at_x, at_y, at_z, sibling = at
    z, c, y, x = where

    begun = []

    def half(i):
        return pl.ds(pl.multiple_of(i * S.half, 8), S.half)

    def part(i):
        return pl.ds(pl.multiple_of((c * P.nx + i) * S.part, 8), S.part)

    def piece(i):
        return pl.ds(pl.multiple_of(i * S.piece, 8), S.piece)

    def begin(copies):
        for copy in copies:
            copy.start()
        while begun:
            begun.pop().wait_send()
        begun.extend(copies)
        return copies

    copies = begin([remote(p.at[half(1 - c)], rc, cs.at[0], cd.at[0], sibling)])
    if S.padded > S.part:
        hx[pl.ds(S.part, S.padded - S.part), :] = jnp.zeros((S.padded - S.part, BLOCK), jnp.float32)
    yield True
    copies[0].wait_recv()
    p[half(c), :] = p[half(c), :] + rc[...]

    copies = begin([remote(p.at[part((x + d) % P.nx)], rx.at[d - 1], ss.at[d - 1], sd.at[d - 1], at_x(d))
                    for d in range(1, P.nx)])
    yield True
    total = p[part(x), :]
    for d, copy in enumerate(copies):
        copy.wait_recv()
        total = total + rx[d]
    hx[pl.ds(0, S.part), :] = total

    copies = begin([remote(hx.at[piece((y + d) % P.ny)], ry.at[d - 1], ys.at[d - 1], yd.at[d - 1], at_y(d))
                    for d in range(1, P.ny)])
    yield True
    total = hx[piece(y), :]
    for d, copy in enumerate(copies):
        copy.wait_recv()
        total = total + ry[d]
    hy[...] = total

    copies = begin([remote(hy, rz.at[z], zs.at[d - 1], zd.at[d - 1], at_z(d)) for d in range(1, P.nz)])
    rz[z] = total
    yield True
    for copy in copies:
        copy.wait_recv()
    total = rz[0]
    for i in range(1, P.nz):
        total = total + rz[i]
    gy[piece(y), :] = total

    copies = begin([remote(gy.at[piece(y)], gy.at[piece(y)], yas.at[d - 1], yad.at[d - 1], at_y(d))
                    for d in range(1, P.ny)])
    yield True
    for copy in copies:
        copy.wait_recv()
    copies = begin([remote(gy.at[pl.ds(0, S.part)], o.at[part(x)], xas.at[d - 1], xad.at[d - 1], at_x(d))
                    for d in range(1, P.nx)])
    o[part(x), :] = gy[pl.ds(0, S.part), :]
    yield True
    for copy in copies:
        copy.wait_recv()
    copies = begin([remote(o.at[half(c)], o.at[half(c)], cas.at[0], cad.at[0], sibling)])
    yield True
    copies[0].wait_recv()
    for copy in begun:
        copy.wait_send()


def filter_and_gram(plan, weights, record):
    P = plan
    f32, dma = jnp.float32, pltpu.SemaphoreType.DMA
    return pl.pallas_call(
        functools.partial(gather_body, plan),
        out_shape=(
            jax.ShapeDtypeStruct((P.time, P.width), f32),
            jax.ShapeDtypeStruct((len(ORDER) * BLOCK, BLOCK), f32),
        ),
        in_specs=[pl.BlockSpec(memory_space=pltpu.HBM)] * 2,
        out_specs=(pl.BlockSpec(memory_space=pl.ANY), pl.BlockSpec(memory_space=pltpu.VMEM)),
        scratch_shapes=[
            pltpu.SMEM((P.taps,), f32),
            pltpu.VMEM((P.time, P.width), f32),
            dma((P.chunks,)),
            pltpu.VMEM((P.time, P.width), f32),
            pltpu.VMEM((BLOCK, 3 * BLOCK), f32),
            pltpu.VMEM((3, 256, 256), f32),
            dma, dma((P.chunks, P.tm - 1)), dma((P.chunks,)), dma((P.chunks,)),
            *[b for S in P.streams for b in S.buffers(P)],
        ],
        compiler_params=pltpu.CompilerParams(
            collective_id=0, has_side_effects=True, vmem_limit_bytes=52000 << 10),
        name="gather_filter_gram",
    )(weights, record)


def solution(mesh):
    def per_device(record, weights):
        rows, width = record.shape[0], record.shape[1] // mesh.shape["tm"]
        plan = Plan(mesh, ALONG_X, rows, width, weights.shape[0])
        fx, gram = filter_and_gram(plan, weights, record)
        points = width * mesh.shape["tm"] * mesh.shape["space"]
        lower, basis = factor_and_solve(gram, fx, points)
        return lower, basis.reshape(plan.time, 1, width)

    return jax.shard_map(
        per_device,
        mesh=mesh,
        in_specs=(P("tm", "space"), P()),
        out_specs=(P(), P(None, "space", "tm")),
        check_vma=False,
    )
```

```python
import functools
import jax
import jax.numpy as jnp
from jax import lax
from jax.experimental import pallas as pl
from jax.experimental.pallas import tpu as pltpu
from jax.sharding import PartitionSpec as P

MESH = pl.DeviceIdType.MESH
ALONG_X = 4
B = 128
OFF = (0, 4, 7, 9)
HI = lax.Precision.HIGHEST


def dot(a, b, dims=((1,), (0,))):
    return lax.dot_general(a, b, (dims, ((), ())), precision=HI, preferred_element_type=jnp.float32)


def recip(d):
    return pl.reciprocal(d, approx=True)


def rsq(d):
    r = lax.rsqrt(d)
    return r


def factor128(rows, cs, gs):
    n = len(rows)
    lane = lax.broadcasted_iota(jnp.int32, (8, B), 1)
    sub = lax.broadcasted_iota(jnp.int32, (8, B), 0)
    m = list(rows)
    upper, inverse = [], []
    for v in range(n):
        j = 8 * v
        g = m[v]
        col = [jnp.broadcast_to(g[:, j + k : j + k + 1], (8, B)) for k in range(8)]
        p = {}
        o = v % 2
        gs[o] = g
        for k in range(8):
            cs[o, k] = col[k]
        for k in range(8):
            for l in range(k, 8):
                p[l, k] = jnp.broadcast_to(cs[o, k, pl.ds(l, 1), :], (8, B))
        ra = [jnp.broadcast_to(gs[o, pl.ds(l, 1), :], (8, B)) for l in range(8)]
        inside = (lane >= j) & (lane < j + 8)
        ri = [jnp.where(inside, jnp.where(lane == j + l, 1.0, 0.0), ra[l]) for l in range(8)]
        piv, n0, n1 = [None] * 8, {}, {}
        qa = [None] * 8
        for k in range(0, 8, 2):
            e = k + 1
            det = p[k, k] * p[e, e] - p[e, k] * p[e, k]
            rd = recip(det)
            i00, i10, i11 = p[e, e] * rd, -p[e, k] * rd, p[k, k] * rd
            for l in range(k + 2, 8):
                n0[l, k] = p[l, k] * i00 + p[l, e] * i10
                n1[l, k] = p[l, k] * i10 + p[l, e] * i11
            for c in range(k + 2, 8):
                for l in range(c, 8):
                    p[l, c] = p[l, c] - (n0[l, k] * p[c, k] + n1[l, k] * p[c, e])
            for l in range(k + 2, 8):
                ra[l] = ra[l] - (n0[l, k] * ra[k] + n1[l, k] * ra[e])
                ri[l] = ri[l] - (n0[l, k] * ri[k] + n1[l, k] * ri[e])
            qa[k] = i00 * ri[k] + i10 * ri[e]
            qa[e] = i10 * ri[k] + i11 * ri[e]
            first = recip(p[k, k])
            mult = p[e, k] * first
            ra[e] = ra[e] - mult * ra[k]
            ri[e] = ri[e] - mult * ri[k]
            p[e, e] = det * first
        q = list(qa)
        for k in (4, 2, 0):
            for l in range(7, k + 1, -1):
                q[k] = q[k] - n0[l, k] * q[l]
                q[k + 1] = q[k + 1] - n1[l, k] * q[l]
        for i in range(v + 1, n):
            ci = [jnp.broadcast_to(m[i][:, j + k : j + k + 1], (8, B)) for k in range(8)]
            t = jnp.where(inside, 0.0, m[i])
            s1 = ci[0] * q[0] + ci[1] * q[1]
            s2 = ci[2] * q[2] + ci[3] * q[3]
            s3 = ci[4] * q[4] + ci[5] * q[5]
            s4 = ci[6] * q[6] + ci[7] * q[7]
            m[i] = t - ((s1 + s2) + (s3 + s4))
        u = jnp.zeros((8, B), jnp.float32)
        w = u
        for l in range(8):
            r = rsq(p[l, l])
            u = jnp.where(sub == l, ra[l] * r, u)
            w = jnp.where(sub == l, ri[l] * r, w)
        upper.append(jnp.where(lane >= j + sub, u, 0.0))
        inverse.append(jnp.where(lane <= j + sub, w, 0.0))
    return upper, inverse


def body(scale, g_ref, fx_ref, l_out, y_out, a, u, t, f, cs, gs, l_ref, y_ref, sem):
    eye = lax.broadcasted_iota(jnp.int32, (B, B), 0) == lax.broadcasted_iota(jnp.int32, (B, B), 1)
    across, down, root = [], [], []
    for k in range(4):
        kept = jnp.where(eye, g_ref[pl.ds(OFF[k] * B, B), :] * scale, 0.0)
        across.append(rsq(jnp.sum(kept, axis=0, keepdims=True)))
        column = jnp.sum(kept, axis=1, keepdims=True)
        down.append(rsq(column))
        root.append(column * down[k])
    for k in range(4):
        for i in range(k, 4):
            b = OFF[k] + i - k
            a[b] = (g_ref[pl.ds(b * B, B), :] * scale) * down[i] * across[k]
        f[pl.ds(k * B, B), :] = fx_ref[pl.ds(k * B, B), :] * down[k]
    l_ref[...] = jnp.zeros_like(l_ref)
    copies = []
    wide = f.shape[1] // B

    def leave(k):
        strip, lines = pl.ds(k * B, B), pl.ds(k * B * wide, B * wide)
        for e, (here, there) in enumerate(((l_ref.at[strip], l_out.at[strip]), (y_ref.at[lines], y_out.at[lines]))):
            copy = pltpu.make_async_copy(here, there, sem.at[e, k])
            copy.start()
            copies.append(copy)

    for k in range(4):
        d = OFF[k]
        rows = [a[d, pl.ds(8 * v, 8), :] for v in range(16)]
        up, iv = factor128(rows, cs, gs)
        for v in range(16):
            u[pl.ds(8 * v, 8), :] = up[v]
            t[pl.ds(8 * v, 8), :] = iv[v]
        tk = t[...]
        if k > 0:
            leave(k - 1)
        l_ref[pl.ds(k * B, B), pl.ds(k * B, B)] = u[...].T * root[k]
        low = {}
        for i in range(k + 1, 4):
            low[i] = dot(a[d + i - k], tk, ((1,), (1,)))
            l_ref[pl.ds(i * B, B), pl.ds(k * B, B)] = low[i] * root[i]
            for j in range(k + 1, i + 1):
                e = OFF[j] + i - j
                a[e] = a[e] - dot(low[i], low[j], ((1,), (1,)))
        y = dot(tk, f[pl.ds(k * B, B), :])
        for i in range(k + 1, 4):
            f[pl.ds(i * B, B), :] = f[pl.ds(i * B, B), :] - dot(low[i], y)
        wide = f.shape[1] // B
        for q in range(wide):
            y_ref[pl.ds(k * B * wide + q, B, stride=wide), :] = y[:, q * B : (q + 1) * B]

    leave(3)
    for copy in copies:
        copy.wait()


def factor_and_solve(gram, fx, points):
    rows, cols = fx.shape
    return pl.pallas_call(
        functools.partial(body, 1.0 / points),
        out_shape=(
            jax.ShapeDtypeStruct((rows, rows), jnp.float32),
            jax.ShapeDtypeStruct((rows * cols // B, B), jnp.float32),
        ),
        in_specs=[pl.BlockSpec(memory_space=pltpu.VMEM)] * 2,
        out_specs=(pl.BlockSpec(memory_space=pl.ANY),) * 2,
        scratch_shapes=[
            pltpu.VMEM((10, B, B), jnp.float32),
            pltpu.VMEM((B, B), jnp.float32),
            pltpu.VMEM((B, B), jnp.float32),
            pltpu.VMEM((rows, cols), jnp.float32),
            pltpu.VMEM((2, 8, 8, B), jnp.float32),
            pltpu.VMEM((2, 8, B), jnp.float32),
            pltpu.VMEM((rows, rows), jnp.float32),
            pltpu.VMEM((rows * cols // B, B), jnp.float32),
            pltpu.SemaphoreType.DMA((2, 4)),
        ],
        compiler_params=pltpu.CompilerParams(vmem_limit_bytes=48 << 20),
        name="factor",
    )(gram, fx)


BLOCK = 128
CHUNK = 256
STREAMS = ((0, 4), (4, 3), (7, 3))
READY = ((), (0, 1), (2,))
ORDER = ((0, 0), (1, 0), (2, 0), (3, 0), (1, 1), (2, 1), (3, 1), (2, 2), (3, 2), (3, 3))


class Stream:
    def __init__(self, first, count, plan):
        self.base, self.packed = first * BLOCK, count * BLOCK
        self.half = self.packed // 2
        self.part = self.half // plan.nx
        self.piece = -(-self.part // (8 * plan.ny)) * 8
        self.padded = self.piece * plan.ny

    def buffers(self, plan):
        x, y, z = plan.nx - 1, plan.ny - 1, plan.nz - 1
        shapes = [
            (self.packed, BLOCK), (self.half, BLOCK), (x, self.part, BLOCK), (self.padded, BLOCK),
            (y, self.piece, BLOCK), (self.piece, BLOCK), (plan.nz, self.piece, BLOCK),
            (self.padded, BLOCK), (self.packed, BLOCK)]
        dma = pltpu.SemaphoreType.DMA
        counts = [plan.nx, plan.nx, x, x, y, y, z, z, y, y, x, x, plan.nx, plan.nx]
        return [pltpu.VMEM(shape, jnp.float32) for shape in shapes] + [dma((n,)) for n in counts]


class Plan:
    def __init__(self, mesh, nx, rows, width, taps):
        self.tm, self.space = mesh.shape["tm"], mesh.shape["space"]
        self.nz, self.nx, self.ny = self.tm // 2, nx, self.space // nx
        self.rows, self.width, self.taps = rows, width, taps
        self.time = rows * self.tm
        self.chunks = width // CHUNK
        self.streams = [Stream(first, count, self) for first, count in STREAMS]


def remote(src, dst, send, recv, where):
    return pltpu.make_async_remote_copy(
        src_ref=src, dst_ref=dst, send_sem=send, recv_sem=recv, device_id=where, device_id_type=MESH
    )


def gather_body(plan, w_hbm, x_ref, fx_out, g_ref, w_ref, fx_ref, fs, xr, band, acc, ws, xs, xd, xl, *rest):
    P = plan
    t, s = lax.axis_index("tm"), lax.axis_index("space")
    z, c = t // 2, t % 2
    y, x = s // P.nx, s % P.nx

    def at_tm(i):
        return {"tm": i}

    def at_x(d):
        return {"space": y * P.nx + (x + d) % P.nx}

    def at_y(d):
        return {"space": ((y + d) % P.ny) * P.nx + x}

    def at_z(d):
        return {"tm": ((z + d) % P.nz) * 2 + c}

    sibling = {"tm": z * 2 + (1 - c)}

    weights = pltpu.make_async_copy(w_hbm, w_ref, ws)
    weights.start()
    barrier = pltpu.get_barrier_semaphore()
    for d in range(1, P.tm):
        pl.semaphore_signal(barrier, inc=1, device_id=at_tm((t + d) % P.tm), device_id_type=MESH)
    for d in range(1, P.nx):
        pl.semaphore_signal(barrier, inc=1, device_id=at_x(d), device_id_type=MESH)
    for d in range(1, P.ny):
        pl.semaphore_signal(barrier, inc=1, device_id=at_y(d), device_id_type=MESH)
    pl.semaphore_wait(barrier, (P.tm - 1) + (P.nx - 1) + (P.ny - 1))

    mine = pl.ds(pl.multiple_of(t * P.rows, 8), P.rows)
    steps = sorted(range(1, P.tm), key=lambda d: -min(d, P.tm - d))
    sends, local = [], []
    for h in range(P.chunks):
        there = pl.ds(h * CHUNK, CHUNK)
        for d in steps:
            peer = (t + d) % P.tm
            src = x_ref.at[:, pl.ds(pl.multiple_of(peer * P.width + h * CHUNK, 128), CHUNK)]
            copy = remote(src, xr.at[mine, there], xs.at[h, d - 1], xd.at[h], at_tm(peer))
            copy.start()
            sends.append(copy)
        own = pltpu.make_async_copy(
            x_ref.at[:, pl.ds(pl.multiple_of(t * P.width + h * CHUNK, 128), CHUNK)],
            xr.at[mine, there], xl.at[h])
        own.start()
        local.append(own)

    r = lax.broadcasted_iota(jnp.int32, (BLOCK, 3 * BLOCK), 0)
    q = lax.broadcasted_iota(jnp.int32, (BLOCK, 3 * BLOCK), 1)
    weights.wait()
    tap = q - r - BLOCK + (P.taps - 1) // 2
    f = jnp.zeros((BLOCK, 3 * BLOCK), jnp.float32)
    for k in range(P.taps):
        f = jnp.where(tap == k, w_ref[k], f)
    band[...] = f

    size = len(rest) // len(P.streams)
    held = [rest[i * size : (i + 1) * size] for i in range(len(P.streams))]
    sums = [sum_everywhere(P, S, (at_x, at_y, at_z, sibling), (z, c, y, x), one)
            for S, one in zip(P.streams, held)]
    leaving = []
    nb = P.time // BLOCK
    for h in range(P.chunks):
        there = pl.ds(h * CHUNK, CHUNK)
        local[h].wait()
        others = xr.at[pl.ds(0, P.time - P.rows), there]
        pltpu.make_async_copy(others, others, xd.at[h]).wait()
        for i in range(nb):
            lo, hi = max(i - 1, 0), min(i + 2, nb)
            fx_ref[pl.ds(i * BLOCK, BLOCK), there] = dot(
                band[:, (lo - i + 1) * BLOCK : (hi - i + 1) * BLOCK],
                xr[pl.ds(lo * BLOCK, (hi - lo) * BLOCK), there])
        copy = pltpu.make_async_copy(fx_ref.at[:, there], fx_out.at[:, there], fs.at[h])
        copy.start()
        leaving.append(copy)
        top = fx_ref[pl.ds(0, 256), there]
        low = fx_ref[pl.ds(256, 256), there]
        for e, (u, v) in enumerate(((top, top), (low, top), (low, low))):
            new = dot(u, v, ((1,), (1,)))
            if h > 0:
                new = acc[e] + new
            if h < P.chunks - 1:
                acc[e] = new
                continue
            for n, (i, j) in enumerate(ORDER):
                if ((0, 0), (1, 0), (1, 1))[e] == (i // 2, j // 2):
                    st = max(o for o, S in enumerate(P.streams) if S.base <= n * BLOCK)
                    held[st][0][pl.ds(n * BLOCK - P.streams[st].base, BLOCK), :] = new[
                        (i % 2) * BLOCK : (i % 2 + 1) * BLOCK, (j % 2) * BLOCK : (j % 2 + 1) * BLOCK]
            for o in READY[e]:
                next(sums[o])
    phase = 0
    while sums:
        sums = [one for one in sums if next(one, None) is not None]
        phase += 1
        if phase == 2:
            for done in sends:
                done.wait_send()
            for copy in leaving:
                copy.wait()
    for st, one in zip(P.streams, held):
        g_ref[pl.ds(st.base, st.packed), :] = one[8][...]


def sum_everywhere(P, S, at, where, held):
    (p, rc, rx, hx, ry, hy, rz, gy, o,
     cs, cd, ss, sd, ys, yd, zs, zd, yas, yad, xas, xad, cas, cad) = held
    at_x, at_y, at_z, sibling = at
    z, c, y, x = where

    begun = []

    def part(i, core):
        return pl.ds(pl.multiple_of((core * P.nx + i) * S.part, 8), S.part)

    def piece(i):
        return pl.ds(pl.multiple_of(i * S.piece, 8), S.piece)

    def begin(copies):
        for copy in copies:
            copy.start()
        return went(copies)

    def went(copies):
        while begun:
            begun.pop().wait_send()
        begun.extend(copies)
        return copies

    order = (*range(1, P.nx), 0)
    copies = begin([remote(p.at[part((x + d) % P.nx, 1 - c)], rc.at[pl.ds(d * S.part, S.part)],
                           cs.at[d], cd.at[d], sibling) for d in order])
    if S.padded > S.part:
        hx[pl.ds(S.part, S.padded - S.part), :] = jnp.zeros((S.padded - S.part, BLOCK), jnp.float32)
    yield True

    onward = []
    for d, copy in zip(order, copies):
        copy.wait_recv()
        kept = part((x + d) % P.nx, c)
        p[kept, :] = p[kept, :] + rc[pl.ds(d * S.part, S.part), :]
        if d > 0:
            onward.append(remote(p.at[kept], rx.at[d - 1], ss.at[d - 1], sd.at[d - 1], at_x(d)))
            onward[-1].start()
    copies = went(onward)
    yield True
    total = p[part(x, c), :]
    for d, copy in enumerate(copies):
        copy.wait_recv()
        total = total + rx[d]
    hx[pl.ds(0, S.part), :] = total

    copies = begin([remote(hx.at[piece((y + d) % P.ny)], ry.at[d - 1], ys.at[d - 1], yd.at[d - 1], at_y(d))
                    for d in range(1, P.ny)])
    yield True
    total = hx[piece(y), :]
    for d, copy in enumerate(copies):
        copy.wait_recv()
        total = total + ry[d]
    hy[...] = total

    copies = begin([remote(hy, rz.at[z], zs.at[d - 1], zd.at[d - 1], at_z(d)) for d in range(1, P.nz)])
    rz[z] = total
    yield True
    for copy in copies:
        copy.wait_recv()
    total = rz[0]
    for i in range(1, P.nz):
        total = total + rz[i]
    gy[piece(y), :] = total

    copies = begin([remote(gy.at[piece(y)], gy.at[piece(y)], yas.at[d - 1], yad.at[d - 1], at_y(d))
                    for d in range(1, P.ny)])
    yield True
    for copy in copies:
        copy.wait_recv()
    copies = begin([remote(gy.at[pl.ds(0, S.part)], o.at[part(x, c)], xas.at[d - 1], xad.at[d - 1], at_x(d))
                    for d in range(1, P.nx)])
    o[part(x, c), :] = gy[pl.ds(0, S.part), :]
    onward = [remote(o.at[part(x, c)], o.at[part(x, c)], cas.at[0], cad.at[0], sibling)]
    onward[0].start()
    yield True
    for d, copy in enumerate(copies, 1):
        copy.wait_recv()
        came = o.at[part((x + P.nx - d) % P.nx, c)]
        onward.append(remote(came, came, cas.at[d], cad.at[d], sibling))
        onward[-1].start()
    copies = went(onward)
    yield True
    for copy in copies:
        copy.wait_recv()
    for copy in begun:
        copy.wait_send()


def filter_and_gram(plan, weights, record):
    P = plan
    f32, dma = jnp.float32, pltpu.SemaphoreType.DMA
    return pl.pallas_call(
        functools.partial(gather_body, plan),
        out_shape=(
            jax.ShapeDtypeStruct((P.time, P.width), f32),
            jax.ShapeDtypeStruct((len(ORDER) * BLOCK, BLOCK), f32),
        ),
        in_specs=[pl.BlockSpec(memory_space=pltpu.HBM)] * 2,
        out_specs=(pl.BlockSpec(memory_space=pl.ANY), pl.BlockSpec(memory_space=pltpu.VMEM)),
        scratch_shapes=[
            pltpu.SMEM((P.taps,), f32),
            pltpu.VMEM((P.time, P.width), f32),
            dma((P.chunks,)),
            pltpu.VMEM((P.time, P.width), f32),
            pltpu.VMEM((BLOCK, 3 * BLOCK), f32),
            pltpu.VMEM((3, 256, 256), f32),
            dma, dma((P.chunks, P.tm - 1)), dma((P.chunks,)), dma((P.chunks,)),
            *[b for S in P.streams for b in S.buffers(P)],
        ],
        compiler_params=pltpu.CompilerParams(
            collective_id=0, has_side_effects=True, vmem_limit_bytes=52000 << 10),
        name="gather_filter_gram",
    )(weights, record)


def solution(mesh):
    def per_device(record, weights):
        rows, width = record.shape[0], record.shape[1] // mesh.shape["tm"]
        plan = Plan(mesh, ALONG_X, rows, width, weights.shape[0])
        fx, gram = filter_and_gram(plan, weights, record)
        points = width * mesh.shape["tm"] * mesh.shape["space"]
        lower, basis = factor_and_solve(gram, fx, points)
        return lower, basis.reshape(plan.time, 1, width)

    return jax.shard_map(
        per_device,
        mesh=mesh,
        in_specs=(P("tm", "space"), P()),
        out_specs=(P(), P(None, "space", "tm")),
        check_vma=False,
    )
```
